256 devices in a mesh: section: 16 (over z, x_lo), sp: 16 (over x_hi, y, core).
Axes of the slice: x: 4 (x_hi: 2, x_lo: 2; x = x_hi * 2 + x_lo), y: 4, z: 8, core: 2. Of those that a mesh axis runs over, the one named last changes fastest.
Arguments:
- slots: bfloat16 [16, 256, 3072], P('section', 'sp'), may hold values from -6 to 6
- patch_of_slot: int32 [16], replicated, may hold values from 0 to 15, each once
- step_of_slot: int32 [16], replicated, may hold values from 0 to 26
- modulation: bfloat16 [16, 28, 3, 3072], P('section'), may hold values from -4 to 4
- w_qkv: bfloat16 [16, 3072, 3, 2048], P('section', None, None, 'sp'), may hold values from -0.109375 to 0.109375
- qk_scale: bfloat16 [16, 2, 128], P('section'), may hold values from 0.25 to 4
- w_mlp_in: bfloat16 [16, 3072, 6144], P('section', None, 'sp'), may hold values from -0.109375 to 0.109375
- w_attn_out: bfloat16 [16, 2048, 3072], P('section', 'sp'), may hold values from -0.125 to 0.125
- w_mlp_out: bfloat16 [16, 6144, 3072], P('section', 'sp'), may hold values from -0.078125 to 0.078125
- kv_cache: bfloat16 [16, 2, 4096, 2048], P('section', None, None, 'sp'), may hold values from -130 to 130
Outputs:
- slots_out: bfloat16 [16, 256, 3072], P('section', 'sp')
- kv_cache_out: bfloat16 [16, 2, 4096, 2048], P('section', None, None, 'sp')
The draws below stay inside these ranges and needn't reach their ends.
Inputs may be any that keep to these rules, and one draw needn't show every extreme that they name: `patch_of_slot`: each patch id names exactly one slot.
All inputs are finite; a program needn't handle non-finite values.
Results may differ from the reference program's by a relative error of at most 0.012.
The reference program's roundings to bfloat16 on the way count: a program that leaves them out, or rounds other values in their place, can miss the bound.
Values may be sent and summed in bfloat16 or wider, within the bound.
No kernel may reach another device: no remote copies, remote signals or barrier semaphores. Data moves between devices by JAX's collectives and lax.ppermute only.
A program may use at most 128 MiB of HBM per device.

```python
import math
import jax
import jax.numpy as jnp
from jax import lax

D = 3072
HD = 128
HEADS = 16
FF = 6144
STEPS = 28
ROUNDS = 2
LAYERS = 16
PATCHES = 16
PATCH_ROWS = 256
TOKENS = 4096


def draw_qk_scale(key, part):
    key_b = jax.random.fold_in(jax.random.fold_in(key, 7), 1)
    array_shape = (LAYERS, 2, HD)
    exponent = jax.random.uniform(key_b, array_shape, jnp.float32, -1.3863, 1.3863)
    gains = jnp.exp(exponent)
    return gains.astype(jnp.bfloat16)


def draw_kv_cache(key, part):
    key_a, key_b = jax.random.split(key, 2)
    array_shape = (LAYERS, TOKENS, HEADS * HD)
    keys = jnp.clip(1.5 * jax.random.normal(key_a, array_shape, jnp.float32), -9.0, 9.0)
    values = jnp.clip(jax.random.normal(key_b, array_shape, jnp.float32), -6.0, 6.0)
    return jnp.stack([keys, values], axis=1).astype(jnp.bfloat16)


def plant(drawn, own_key, least, top_value):
    longest = drawn.shape.index(max(drawn.shape))
    spots = []
    for shift in (0, 1):
        where = [jax.random.randint(jax.random.fold_in(own_key, axis), (), 0, length) for axis, length in enumerate(drawn.shape)]
        where[longest] = (where[longest] + shift) % drawn.shape[longest]
        spots.append(tuple(where))
    return drawn.at[spots[0]].set(least).at[spots[1]].set(top_value)


def shard_levels(stream_key, extent, cuts, low, high):
    loudness, own = 1.0, jax.random.fold_in(stream_key, 6)
    for dim, blocks in cuts:
        draws = jnp.exp(jax.random.uniform(jax.random.fold_in(own, dim), (blocks,), jnp.float32, low / len(cuts), high / len(cuts)))
        loudness = loudness * jnp.repeat(draws, extent[dim] // blocks).reshape([-1 if axis == dim else 1 for axis in range(len(extent))])
    return loudness


def normal_values(key, extent, scale, reach, pieces=(), held_as=jnp.bfloat16):
    array = scale * jax.random.normal(key, extent, jnp.float32)
    if pieces:
        array = array * shard_levels(key, extent, pieces, -0.22, 0.18)
    return jnp.clip(array, -reach, reach).astype(held_as)


def setup_inputs(seed: int = 0) -> dict:
    streams_of = jax.random.split(jax.random.key(seed), 11)
    return {
        "slots": normal_values(streams_of[0], (PATCHES, PATCH_ROWS, D), 1.0, 6.0, ((0, 16), (1, 16))),
        "patch_of_slot": jax.random.permutation(streams_of[1], PATCHES).astype(jnp.int32),
        "step_of_slot": plant(jax.random.randint(streams_of[2], (PATCHES,), 0, STEPS - 1), jax.random.fold_in(streams_of[2], 1), 0, (STEPS - 1) - 1).astype(jnp.int32),
        "modulation": normal_values(streams_of[3], (LAYERS, STEPS, 3, D), 0.6, 4.0, ((0, 16),)),
        "w_qkv": normal_values(streams_of[4], (LAYERS, D, 3, HEADS * HD), D ** -0.5, 0.109375, ((0, 16), (3, 16))),
        "qk_scale": draw_qk_scale(jax.random.fold_in(streams_of[10], 71), 0),
        "w_mlp_in": normal_values(streams_of[6], (LAYERS, D, FF), D ** -0.5, 0.109375, ((0, 16), (2, 16))),
        "w_attn_out": normal_values(streams_of[7], (LAYERS, HEADS * HD, D), (HEADS * HD) ** -0.5, 0.125, ((0, 16), (1, 16))),
        "w_mlp_out": normal_values(streams_of[8], (LAYERS, FF, D), FF ** -0.5, 0.078125, ((0, 16), (1, 16))),
        "kv_cache": draw_kv_cache(jax.random.fold_in(streams_of[10], 71), 0),
    }


def head_norm(part, gain):
    rows = part.shape[0]
    wide = part.astype(jnp.float32).reshape(rows, -1, HD)
    power = lax.optimization_barrier(jnp.mean(wide * wide, axis=-1, keepdims=True))
    normed = wide * lax.rsqrt(power + 1e-06) * gain.astype(jnp.float32)
    return normed.astype(jnp.bfloat16).reshape(rows, -1)

def one_block(operands):
    slot, patch_id, timestep, table, qkv_weight, norm_gain, inner_weight, attention_weight, outer_weight, cache = operands
    factors = lax.dynamic_index_in_dim(table, timestep, 0, keepdims=False).astype(jnp.float32)
    wide = slot.astype(jnp.float32)
    center = wide - lax.optimization_barrier(jnp.mean(wide, axis=-1, keepdims=True))
    spread = lax.optimization_barrier(jnp.mean(center * center, axis=-1, keepdims=True))
    normed = (center * lax.rsqrt(spread + 1e-06) * (1.0 + factors[1]) + factors[0]).astype(jnp.bfloat16)
    projected = jnp.einsum('rd,dce->rce', normed.astype(jnp.float32), qkv_weight.astype(jnp.float32)).astype(jnp.bfloat16)
    query_normed = head_norm(projected[:, 0], norm_gain[0])
    key_normed = head_norm(projected[:, 1], norm_gain[1])
    first_row = (patch_id * PATCH_ROWS).astype(jnp.int32)
    keys = lax.dynamic_update_slice_in_dim(cache[0], key_normed, first_row, 0)
    values = lax.dynamic_update_slice_in_dim(cache[1], projected[:, 2], first_row, 0)
    queries = query_normed.astype(jnp.float32).reshape(PATCH_ROWS, HEADS, HD)
    key_heads = keys.astype(jnp.float32).reshape(TOKENS, HEADS, HD)
    value_heads = values.astype(jnp.float32).reshape(TOKENS, HEADS, HD)
    scores = jnp.einsum('rhd,thd->hrt', queries, key_heads) / math.sqrt(HD)
    shifted = jnp.exp(scores - lax.optimization_barrier(jnp.max(scores, axis=-1, keepdims=True)))
    weights = (shifted / lax.optimization_barrier(jnp.sum(shifted, axis=-1, keepdims=True))).astype(jnp.bfloat16)
    attention = jnp.einsum('hrt,thd->rhd', weights.astype(jnp.float32), value_heads).astype(jnp.bfloat16)
    attention = attention.reshape(PATCH_ROWS, HEADS * HD)
    activity = jax.nn.gelu(jnp.dot(normed, inner_weight, preferred_element_type=jnp.float32), approximate=True).astype(jnp.bfloat16)
    branch = jnp.dot(attention, attention_weight, preferred_element_type=jnp.float32) + jnp.dot(activity, outer_weight, preferred_element_type=jnp.float32)
    result = (wide + factors[2] * branch).astype(jnp.bfloat16)
    return (result, jnp.stack([keys, values]))

def reference(slots, patch_of_slot, step_of_slot, modulation, w_qkv, qk_scale, w_mlp_in, w_attn_out, w_mlp_out, kv_cache):
    current = slots
    cache = kv_cache
    patch_ids = patch_of_slot
    timesteps = step_of_slot
    first_slot = (jnp.arange(PATCHES) == 0).astype(jnp.int32)
    for round_id in range(ROUNDS):
        current, cache = lax.map(one_block, (current, patch_ids, timesteps, modulation, w_qkv, qk_scale, w_mlp_in, w_attn_out, w_mlp_out, cache))
        current = jnp.roll(current, 1, axis=0)
        patch_ids = jnp.roll(patch_ids, 1)
        timesteps = jnp.roll(timesteps, 1) + first_slot
    return (current, cache)
```

```python
import math

import jax
import jax.numpy as jnp
from jax import lax
from jax.experimental import pallas as pl
from jax.experimental.pallas import tpu as pltpu
from jax.sharding import PartitionSpec as P

HD = 128
D = 3072
ROWS = 256
TOKENS = 4096
HIDDEN = 384
PIECE = 16
PAIR = 32
HALF = 128
SECTIONS = 16
SPAN = 16
BF = jnp.bfloat16
F32 = jnp.float32
MIB = 1 << 20


def send_core(x):
    return lax.ppermute(x, "sp", [(i, i ^ 1) for i in range(SPAN)])


def send_y(x, by):
    return lax.ppermute(
        x, "sp", [(i, (i & 9) | ((((i >> 1) & 3) + by) % 4) << 1) for i in range(SPAN)]
    )


def send_x(x):
    return lax.ppermute(x, "sp", [(i, i ^ 8) for i in range(SPAN)])


def send_on(x, flip):
    pairs = []
    for s in range(SECTIONS):
        for i in range(SPAN):
            pairs.append((s * SPAN + i, ((s + 1) % SECTIONS) * SPAN + (i ^ flip)))
    return lax.ppermute(x, ("section", "sp"), pairs)


def in_vmem(x):
    return pltpu.with_memory_space_constraint(x, pltpu.VMEM)


def local_call(body, outs, args, scratch=(), limit=16, flops=0, moved=0, name=None, aliases=None):
    specs = []
    given = []
    for kind, arg in args:
        if kind == "smem":
            specs.append(pl.BlockSpec(memory_space=pltpu.SMEM))
            given.append(arg)
        elif kind == "any":
            specs.append(pl.BlockSpec(memory_space=pl.ANY))
            given.append(arg)
        else:
            specs.append(pl.BlockSpec(memory_space=pltpu.VMEM))
            given.append(in_vmem(arg))
    out_specs = []
    out_shape = []
    for kind, shape, dtype in outs:
        if kind == "any":
            out_specs.append(pl.BlockSpec(memory_space=pl.ANY))
            out_shape.append(jax.ShapeDtypeStruct(shape, dtype))
        else:
            out_specs.append(pl.BlockSpec(memory_space=pltpu.VMEM))
            out_shape.append(pltpu.VMEM(shape, dtype))
    return pl.pallas_call(
        body,
        out_shape=out_shape,
        in_specs=specs,
        out_specs=out_specs,
        scratch_shapes=list(scratch),
        input_output_aliases=aliases or {},
        compiler_params=pltpu.CompilerParams(vmem_limit_bytes=limit * MIB),
        cost_estimate=pl.CostEstimate(flops=flops, bytes_accessed=moved, transcendentals=0),
        name=name,
    )(*given)


def layer_norm(wide, factors):
    center = wide - jnp.mean(wide, axis=-1, keepdims=True)
    spread = jnp.mean(center * center, axis=-1, keepdims=True)
    shift = factors[0:1, :].astype(F32)
    scale = factors[1:2, :].astype(F32)
    return (center * lax.rsqrt(spread + 1e-06) * (1.0 + scale) + shift).astype(BF)


def start_body(where, own, other, factors, normed, kept):
    xh = where[1]
    mine = pl.multiple_of(xh * PIECE, PIECE)
    theirs = pl.multiple_of((1 - xh) * PIECE, PIECE)
    kept[pl.ds(mine, PIECE), :] = own[...]
    kept[pl.ds(theirs, PIECE), :] = other[...]
    table = factors[...]
    normed[pl.ds(mine, PIECE), :] = layer_norm(own[...].astype(F32), table)
    normed[pl.ds(theirs, PIECE), :] = layer_norm(other[...].astype(F32), table)


def head_norm(part, gain):
    wide = part.astype(F32)
    power = jnp.mean(wide * wide, axis=-1, keepdims=True)
    return (wide * lax.rsqrt(power + 1e-06) * gain.astype(F32)).astype(BF)


def gelu(x):
    return jax.nn.gelu(x, approximate=True)


def block_body(
    where, n0, n1, n2, n3, s0, s1, s2, s3, w1, w2, gains, cache, new_cache, joined, partial,
    rows, kv, scores, sems,
):
    patch = pl.multiple_of(where[0] * ROWS, ROWS)
    xh, y, core = where[1], where[2], where[3]
    reads = [
        pltpu.make_async_copy(cache.at[i], kv.at[i], sems.at[i]) for i in range(2)
    ]
    for r in reads:
        r.start()
    for i, piece in enumerate((n0, n1, n2, n3, s0, s1, s2, s3)):
        rows[i * PAIR:(i + 1) * PAIR, :] = piece[...]
    h = rows[...]
    qk = jnp.dot(h, w1[:, 0:256], preferred_element_type=F32).astype(BF)
    vm = jnp.dot(h, w1[:, 256:512], preferred_element_type=F32)
    mm = jnp.dot(h, w1[:, 512:768], preferred_element_type=F32)
    query = head_norm(qk[:, :HD], gains[0:1, :])
    key = head_norm(qk[:, HD:], gains[1:2, :])
    value = vm[:, :HD].astype(BF)
    joined[:, HD:2 * HD] = gelu(vm[:, HD:]).astype(BF)
    joined[:, 2 * HD:] = gelu(mm).astype(BF)
    for r in reads:
        r.wait()
    for dc in range(2):
        for dy in range(4):
            for x in range(2):
                at = (dc * 4 + dy) * PAIR + x * PIECE
                row = x * HALF + lax.rem(y + dy, 4) * PAIR + jnp.where(core == dc, 0, PIECE)
                to = pl.multiple_of(patch + row, PIECE)
                kv[0, pl.ds(to, PIECE), :] = key[at:at + PIECE, :]
                kv[1, pl.ds(to, PIECE), :] = value[at:at + PIECE, :]
    writes = [
        pltpu.make_async_copy(
            kv.at[i, pl.ds(patch, ROWS)], new_cache.at[i, pl.ds(patch, ROWS)], sems.at[2 + i]
        )
        for i in range(2)
    ]
    for w in writes:
        w.start()
    step = 512
    top = None
    for j in range(TOKENS // step):
        s = lax.dot_general(
            query, kv[0, j * step:(j + 1) * step, :], (((1,), (1,)), ((), ())),
            preferred_element_type=F32,
        ) * (1.0 / math.sqrt(HD))
        scores[:, j * step:(j + 1) * step] = s
        best = jnp.max(s, axis=-1, keepdims=True)
        top = best if top is None else jnp.maximum(top, best)
    total = None
    mixed = None
    for j in range(TOKENS // step):
        e = jnp.exp(scores[:, j * step:(j + 1) * step] - top)
        t = jnp.sum(e, axis=-1, keepdims=True)
        m = jnp.dot(
            e.astype(BF), kv[1, j * step:(j + 1) * step, :], preferred_element_type=F32
        )
        total = t if total is None else total + t
        mixed = m if mixed is None else mixed + m
    joined[:, 0:HD] = (mixed / total).astype(BF)
    theirs = joined[HALF:, :]
    for j in range(D // 256):
        partial[:, j * 256:(j + 1) * 256] = jnp.dot(
            theirs, w2[:, j * 256:(j + 1) * 256], preferred_element_type=F32
        ).astype(BF)
    for w in writes:
        w.wait()


def own_body(joined, w2, partial):
    mine = joined[:HALF, :]
    for j in range(D // 256):
        partial[:, j * 256:(j + 1) * 256] = jnp.dot(
            mine, w2[:, j * 256:(j + 1) * 256], preferred_element_type=F32
        )


def pair_body(mine, came, o0, o1, o2, o3):
    o0[...] = mine[0:PAIR, :] + came[0:PAIR, :].astype(F32)
    for i, o in ((1, o1), (2, o2), (3, o3)):
        a, b = i * PAIR, (i + 1) * PAIR
        o[...] = (mine[a:b, :] + came[a:b, :].astype(F32)).astype(BF)


def column_body(mine, r1, r2, r3, factors, out):
    total = mine[...] + r1[...].astype(F32) + (r2[...].astype(F32) + r3[...].astype(F32))
    out[...] = (factors[2:3, :].astype(F32) * total).astype(BF)


def last_column_body(where, mine, r1, r2, r3, factors, here, there):
    xh = where[1]
    gate = factors[2:3, :].astype(F32)
    for out, at in ((here, xh), (there, 1 - xh)):
        rows = pl.ds(pl.multiple_of(at * PIECE, PIECE), PIECE)
        total = mine[rows, :] + r1[rows, :].astype(F32)
        total = total + (r2[rows, :].astype(F32) + r3[rows, :].astype(F32))
        out[...] = (gate * total).astype(BF)


def next_body(where, kept, p0, p1, factors, normed, own):
    xh = where[1]
    new = (kept[...].astype(F32) + (p0[...].astype(F32) + p1[...].astype(F32))).astype(BF)
    wide = new.astype(F32)
    normed[...] = layer_norm(wide, factors[...])
    own[...] = jnp.where(xh == 0, new[:PIECE, :], new[PIECE:, :])


def final_body(kept, p0, p1, out):
    out[...] = (kept[...].astype(F32) + (p0[...].astype(F32) + p1[...].astype(F32))).astype(BF)


def block(normed, where, w1, w2, gains, cache):
    core_parts = [send_core(normed)]
    parts = [normed] + [send_y(normed, -dy) for dy in (1, 2, 3)]
    core_parts += [send_core(p) for p in parts[1:]]
    new_cache, joined, partial = local_call(
        block_body,
        [("any", cache.shape, BF), ("vmem", (ROWS, 4 * HD), BF), ("vmem", (HALF, D), BF)],
        [("smem", where)] + [("vmem", p) for p in parts + core_parts]
        + [("vmem", w1), ("vmem", w2), ("vmem", gains), ("any", cache)],
        scratch=[
            pltpu.VMEM((ROWS, D), BF),
            pltpu.VMEM((2, TOKENS, HD), BF),
            pltpu.VMEM((ROWS, TOKENS), F32),
            pltpu.SemaphoreType.DMA((4,)),
        ],
        limit=24,
        flops=2_200_000_000,
        moved=12_000_000,
        name="block",
        aliases={12: 0},
    )
    came = send_core(partial)
    (mine,) = local_call(
        own_body,
        [("vmem", (HALF, D), F32)],
        [("vmem", joined), ("vmem", w2)],
        flops=400_000_000,
        moved=4_700_000,
        name="own_half",
    )
    o0, o1, o2, o3 = local_call(
        pair_body,
        [("vmem", (PAIR, D), F32)] + [("vmem", (PAIR, D), BF)] * 3,
        [("vmem", mine), ("vmem", came)],
        flops=400_000,
        moved=3_000_000,
        name="pair_sum",
    )
    return (o0, send_y(o1, 1), send_y(o2, 2), send_y(o3, 3)), new_cache


def labels(patch_of_slot, step_of_slot, section_id, round_id):
    anchor = section_id - round_id
    wrapped = (anchor < 0).astype(jnp.int32)
    anchor = anchor + wrapped * SECTIONS
    patch_id = lax.dynamic_index_in_dim(patch_of_slot, anchor, 0, keepdims=False)
    timestep = lax.dynamic_index_in_dim(step_of_slot, anchor, 0, keepdims=False) + wrapped
    return patch_id, timestep


def shards(
    slots,
    patch_of_slot,
    step_of_slot,
    modulation,
    w_qkv,
    qk_scale,
    w_mlp_in,
    w_attn_out,
    w_mlp_out,
    kv_cache,
):
    section_id = lax.axis_index("section")
    place = lax.axis_index("sp")
    xh, y, core = place // 8, (place // 2) % 4, place % 2
    own = slots[0]
    other = send_x(own)
    where, factors = [], []
    for r in range(2):
        patch, step = labels(patch_of_slot, step_of_slot, section_id, r)
        where.append(jnp.stack([patch, xh, y, core]).astype(jnp.int32))
        factors.append(lax.dynamic_index_in_dim(modulation[0], step, 0, keepdims=False))
    w1 = jnp.concatenate([w_qkv[0].reshape(D, 3 * HD), w_mlp_in[0]], axis=1)
    w2 = jnp.concatenate([w_attn_out[0], w_mlp_out[0]], axis=0)
    gains = qk_scale[0]
    cache = kv_cache[0]

    normed, kept = local_call(
        start_body,
        [("vmem", (PAIR, D), BF)] * 2,
        [("smem", where[0]), ("vmem", own), ("vmem", other), ("vmem", factors[0])],
        flops=1_000_000,
        moved=400_000,
        name="norm_first",
    )
    kept = send_on(kept, 0)
    sums, cache = block(normed, where[0], w1, w2, gains, cache)
    (out,) = local_call(
        column_body,
        [("vmem", (PAIR, D), BF)],
        [("vmem", a) for a in sums] + [("vmem", factors[0])],
        flops=400_000,
        moved=1_200_000,
        name="column_sum",
    )
    p0, p1 = send_on(out, 0), send_on(out, 8)
    normed, kept = local_call(
        next_body,
        [("vmem", (PAIR, D), BF), ("vmem", (PIECE, D), BF)],
        [("smem", where[1])] + [("vmem", a) for a in (kept, p0, p1, factors[1])],
        flops=1_000_000,
        moved=800_000,
        name="norm_next",
    )
    kept = send_on(kept, 0)
    sums, cache = block(normed, where[1], w1, w2, gains, cache)
    here, there = local_call(
        last_column_body,
        [("vmem", (PIECE, D), BF)] * 2,
        [("smem", where[1])] + [("vmem", a) for a in sums] + [("vmem", factors[1])],
        flops=400_000,
        moved=1_200_000,
        name="column_last",
    )
    p0, p1 = send_on(here, 0), send_on(there, 8)
    (out,) = local_call(
        final_body,
        [("vmem", (PIECE, D), BF)],
        [("vmem", a) for a in (kept, p0, p1)],
        flops=400_000,
        moved=400_000,
        name="residual_last",
    )
    return out[None], cache[None]


def solution(mesh):
    return jax.shard_map(
        shards,
        mesh=mesh,
        in_specs=(
            P("section", "sp", None),
            P(),
            P(),
            P("section", None, None, None),
            P("section", None, None, "sp"),
            P("section", None, None),
            P("section", None, "sp"),
            P("section", "sp", None),
            P("section", "sp", None),
            P("section", None, None, "sp"),
        ),
        out_specs=(P("section", "sp", None), P("section", None, None, "sp")),
        check_vma=False,
    )
```

```python
import functools
import math

import jax
import jax.numpy as jnp
from jax import lax
from jax.experimental import pallas as pl
from jax.experimental.pallas import tpu as pltpu
from jax.sharding import PartitionSpec as P

HD = 128
D = 3072
ROWS = 256
TOKENS = 4096
HIDDEN = 384
PIECE = 16
PAIR = 32
HALF = 128
SECTIONS = 16
SPAN = 16
BF = jnp.bfloat16
F32 = jnp.float32
MIB = 1 << 20


def send_core(x):
    return lax.ppermute(x, "sp", [(i, i ^ 1) for i in range(SPAN)])


def send_y(x, by):
    return lax.ppermute(
        x, "sp", [(i, (i & 9) | ((((i >> 1) & 3) + by) % 4) << 1) for i in range(SPAN)]
    )


def send_x(x):
    return lax.ppermute(x, "sp", [(i, i ^ 8) for i in range(SPAN)])


def send_on(x, flip):
    pairs = []
    for s in range(SECTIONS):
        for i in range(SPAN):
            pairs.append((s * SPAN + i, ((s + 1) % SECTIONS) * SPAN + (i ^ flip)))
    return lax.ppermute(x, ("section", "sp"), pairs)


def in_vmem(x):
    return pltpu.with_memory_space_constraint(x, pltpu.VMEM)


def local_call(body, outs, args, scratch=(), limit=16, flops=0, moved=0, name=None, aliases=None):
    specs = []
    given = []
    for kind, arg in args:
        if kind == "smem":
            specs.append(pl.BlockSpec(memory_space=pltpu.SMEM))
            given.append(arg)
        elif kind == "any":
            specs.append(pl.BlockSpec(memory_space=pl.ANY))
            given.append(arg)
        elif kind == "hbm":
            specs.append(pl.BlockSpec(memory_space=pltpu.HBM))
            given.append(pltpu.with_memory_space_constraint(arg, pltpu.HBM))
        else:
            specs.append(pl.BlockSpec(memory_space=pltpu.VMEM))
            given.append(in_vmem(arg))
    out_specs = []
    out_shape = []
    for kind, shape, dtype in outs:
        if kind in ("any", "hbm"):
            space = pl.ANY if kind == "any" else pltpu.VMEM
            out_specs.append(pl.BlockSpec(memory_space=space))
            out_shape.append(jax.ShapeDtypeStruct(shape, dtype))
        else:
            out_specs.append(pl.BlockSpec(memory_space=pltpu.VMEM))
            out_shape.append(pltpu.VMEM(shape, dtype))
    return pl.pallas_call(
        body,
        out_shape=out_shape,
        in_specs=specs,
        out_specs=out_specs,
        scratch_shapes=list(scratch),
        input_output_aliases=aliases or {},
        compiler_params=pltpu.CompilerParams(vmem_limit_bytes=limit * MIB),
        cost_estimate=pl.CostEstimate(flops=flops, bytes_accessed=moved, transcendentals=0),
        name=name,
    )(*given)


def layer_norm(wide, factors):
    center = wide - jnp.mean(wide, axis=-1, keepdims=True)
    spread = jnp.mean(center * center, axis=-1, keepdims=True)
    shift = factors[0:1, :].astype(F32)
    scale = factors[1:2, :].astype(F32)
    return (center * lax.rsqrt(spread + 1e-06) * (1.0 + scale) + shift).astype(BF)


def start_body(where, own, other, factors, fetched, normed, kept):
    xh = where[1]
    mine = pl.multiple_of(xh * PIECE, PIECE)
    theirs = pl.multiple_of((1 - xh) * PIECE, PIECE)
    kept[pl.ds(mine, PIECE), :] = own[...]
    kept[pl.ds(theirs, PIECE), :] = other[...]
    table = factors[...]
    normed[pl.ds(mine, PIECE), :] = layer_norm(own[...].astype(F32), table)
    normed[pl.ds(theirs, PIECE), :] = layer_norm(other[...].astype(F32), table)


def fetch_body(w_qkv, w_mlp_in, w_attn_out, w_mlp_out, cache, w1, w2, kv, sems):
    pairs = [(w_qkv.at[i], w1.at[:, i * HD:(i + 1) * HD]) for i in range(3)]
    pairs += [(w_mlp_in, w1.at[:, 3 * HD:]), (w_attn_out, w2.at[:HD, :]), (w_mlp_out, w2.at[HD:, :])]
    pairs += [(cache.at[i], kv.at[i]) for i in range(2)]
    copies = [pltpu.make_async_copy(a, b, sems.at[i]) for i, (a, b) in enumerate(pairs)]
    for c in copies:
        c.start()
    for c in copies:
        c.wait()


def head_norm(part, gain):
    wide = part.astype(F32)
    power = jnp.mean(wide * wide, axis=-1, keepdims=True)
    return (wide * lax.rsqrt(power + 1e-06) * gain.astype(F32)).astype(BF)


def gelu(x):
    return jax.nn.gelu(x, approximate=True)


def block_body(
    last, where, n0, n2, n1, n3, s0, s2, s1, s3, w1, w2, gains, old, *rest,
):
    if last:
        kv, joined, partial, new_cache, rows, scores, sems = rest
    else:
        passing, kv, joined, partial, rows, scores = rest
    patch = pl.multiple_of(where[4 if last else 0] * ROWS, ROWS)
    y, core = where[2], where[3]
    for i, piece in enumerate((n0, n1, n2, n3, s0, s1, s2, s3)):
        rows[i * PAIR:(i + 1) * PAIR, :] = piece[...]
    h = rows[...]
    qk = jnp.dot(h, w1[:, 0:256], preferred_element_type=F32).astype(BF)
    vm = jnp.dot(h, w1[:, 256:512], preferred_element_type=F32)
    mm = jnp.dot(h, w1[:, 512:768], preferred_element_type=F32)
    query = head_norm(qk[:, :HD], gains[0:1, :])
    key = head_norm(qk[:, HD:], gains[1:2, :])
    value = vm[:, :HD].astype(BF)
    joined[:, HD:2 * HD] = gelu(vm[:, HD:]).astype(BF)
    joined[:, 2 * HD:] = gelu(mm).astype(BF)
    for dc in range(2):
        for dy in range(4):
            for x in range(2):
                at = (dc * 4 + dy) * PAIR + x * PIECE
                row = x * HALF + lax.rem(y + dy, 4) * PAIR + jnp.where(core == dc, 0, PIECE)
                to = pl.multiple_of(patch + row, PIECE)
                kv[0, pl.ds(to, PIECE), :] = key[at:at + PIECE, :]
                kv[1, pl.ds(to, PIECE), :] = value[at:at + PIECE, :]
    writes = []
    if last:
        writes = [pltpu.make_async_copy(kv.at[i], new_cache.at[i], sems.at[i]) for i in range(2)]
    for w in writes:
        w.start()
    step = 512
    top = None
    for j in range(TOKENS // step):
        s = lax.dot_general(
            query, kv[0, j * step:(j + 1) * step, :], (((1,), (1,)), ((), ())),
            preferred_element_type=F32,
        ) * (1.0 / math.sqrt(HD))
        scores[:, j * step:(j + 1) * step] = s
        best = jnp.max(s, axis=-1, keepdims=True)
        top = best if top is None else jnp.maximum(top, best)
    total = None
    mixed = None
    for j in range(TOKENS // step):
        e = jnp.exp(scores[:, j * step:(j + 1) * step] - top)
        t = jnp.sum(e, axis=-1, keepdims=True)
        m = jnp.dot(
            e.astype(BF), kv[1, j * step:(j + 1) * step, :], preferred_element_type=F32
        )
        total = t if total is None else total + t
        mixed = m if mixed is None else mixed + m
    joined[:, 0:HD] = (mixed / total).astype(BF)
    theirs = joined[HALF:, :]
    for j in range(D // 256):
        partial[:, j * 256:(j + 1) * 256] = jnp.dot(
            theirs, w2[:, j * 256:(j + 1) * 256], preferred_element_type=F32
        ).astype(BF)
    for w in writes:
        w.wait()


def own_body(joined, w2, partial):
    mine = joined[:HALF, :]
    for j in range(D // 256):
        partial[:, j * 256:(j + 1) * 256] = jnp.dot(
            mine, w2[:, j * 256:(j + 1) * 256], preferred_element_type=F32
        )


def pair_body(mine, came, o0, o1, o2, o3):
    o0[...] = mine[0:PAIR, :] + came[0:PAIR, :].astype(F32)
    for i, o in ((1, o1), (2, o2), (3, o3)):
        a, b = i * PAIR, (i + 1) * PAIR
        o[...] = (mine[a:b, :] + came[a:b, :].astype(F32)).astype(BF)


def column_body(mine, r1, r3, r2, factors, out):
    total = mine[...] + r1[...].astype(F32) + (r2[...].astype(F32) + r3[...].astype(F32))
    out[...] = (factors[2:3, :].astype(F32) * total).astype(BF)


def last_column_body(where, mine, r1, r3, r2, factors, here, there):
    xh = where[1]
    gate = factors[2:3, :].astype(F32)
    for out, at in ((here, xh), (there, 1 - xh)):
        rows = pl.ds(pl.multiple_of(at * PIECE, PIECE), PIECE)
        total = mine[rows, :] + r1[rows, :].astype(F32)
        total = total + (r2[rows, :].astype(F32) + r3[rows, :].astype(F32))
        out[...] = (gate * total).astype(BF)


def next_body(where, kept, p0, p1, factors, normed, own):
    xh = where[1]
    new = (kept[...].astype(F32) + (p0[...].astype(F32) + p1[...].astype(F32))).astype(BF)
    wide = new.astype(F32)
    normed[...] = layer_norm(wide, factors[...])
    own[...] = jnp.where(xh == 0, new[:PIECE, :], new[PIECE:, :])


def final_body(kept, p0, p1, out):
    out[...] = (kept[...].astype(F32) + (p0[...].astype(F32) + p1[...].astype(F32))).astype(BF)


def block(last, normed, passing, where, w1, w2, gains, kv):
    core_parts = [send_core(normed)]
    n2 = send_y(normed, 2)
    n3 = send_y(normed, 1)
    n1 = send_y(normed, 3)
    core_parts += [send_core(p) for p in (n2, n1, n3)]
    outs = [("vmem", kv.shape, BF), ("vmem", (ROWS, 4 * HD), BF), ("vmem", (HALF, D), BF)]
    scratch = [pltpu.VMEM((ROWS, D), BF), pltpu.VMEM((ROWS, TOKENS), F32)]
    if last:
        outs.append(("any", kv.shape, BF))
        scratch.append(pltpu.SemaphoreType.DMA((2,)))
    kv, joined, partial, *cache = local_call(
        functools.partial(block_body, last),
        outs,
        [("smem", where)] + [("vmem", p) for p in [normed, n2, n1, n3] + core_parts]
        + [("vmem", w1), ("vmem", w2), ("vmem", gains), ("vmem", kv)]
        + ([] if last else [("any", passing)]),
        scratch=scratch,
        limit=24,
        flops=2_200_000_000,
        moved=12_000_000,
        name="block",
        aliases={12: 0},
    )
    came = send_core(partial)
    (mine,) = local_call(
        own_body,
        [("vmem", (HALF, D), F32)],
        [("vmem", joined), ("vmem", w2)],
        flops=400_000_000,
        moved=4_700_000,
        name="own_half",
    )
    o0, o1, o2, o3 = local_call(
        pair_body,
        [("vmem", (PAIR, D), F32)] + [("vmem", (PAIR, D), BF)] * 3,
        [("vmem", mine), ("vmem", came)],
        flops=400_000,
        moved=3_000_000,
        name="pair_sum",
    )
    r2 = send_y(o2, 2)
    r1 = send_y(o1, 1)
    r3 = send_y(o3, 3)
    return (o0, r1, r3, r2), kv, cache


def labels(patch_of_slot, step_of_slot, section_id, round_id):
    anchor = section_id - round_id
    wrapped = (anchor < 0).astype(jnp.int32)
    anchor = anchor + wrapped * SECTIONS
    patch_id = lax.dynamic_index_in_dim(patch_of_slot, anchor, 0, keepdims=False)
    timestep = lax.dynamic_index_in_dim(step_of_slot, anchor, 0, keepdims=False) + wrapped
    return patch_id, timestep


def shards(
    slots,
    patch_of_slot,
    step_of_slot,
    modulation,
    w_qkv,
    qk_scale,
    w_mlp_in,
    w_attn_out,
    w_mlp_out,
    kv_cache,
):
    section_id = lax.axis_index("section")
    place = lax.axis_index("sp")
    xh, y, core = place // 8, (place // 2) % 4, place % 2
    own = slots[0]
    other = send_x(own)
    labelled = [labels(patch_of_slot, step_of_slot, section_id, r) for r in range(2)]
    where = jnp.stack([labelled[0][0], xh, y, core, labelled[1][0]]).astype(jnp.int32)
    factors = [
        lax.dynamic_index_in_dim(modulation[0], step, 0, keepdims=False) for _, step in labelled
    ]
    gains = qk_scale[0]
    w1, w2, kv = local_call(
        fetch_body,
        [("vmem", (D, 6 * HD), BF), ("vmem", (4 * HD, D), BF), ("vmem", (2, TOKENS, HD), BF)],
        [
            ("hbm", jnp.transpose(w_qkv[0], (1, 0, 2))),
            ("hbm", w_mlp_in[0]),
            ("hbm", w_attn_out[0]),
            ("hbm", w_mlp_out[0]),
            ("hbm", kv_cache[0]),
        ],
        scratch=[pltpu.SemaphoreType.DMA((8,))],
        flops=0,
        moved=10_000_000,
        name="fetch",
    )

    normed, kept = local_call(
        start_body,
        [("vmem", (PAIR, D), BF)] * 2,
        [("smem", where), ("vmem", own), ("vmem", other), ("vmem", factors[0])]
        + [("any", w1)],
        flops=1_000_000,
        moved=400_000,
        name="norm_first",
    )
    kept = send_on(kept, 0)
    sums, kv, _ = block(False, normed, kept, where, w1, w2, gains, kv)
    (out,) = local_call(
        column_body,
        [("vmem", (PAIR, D), BF)],
        [("vmem", a) for a in sums] + [("vmem", factors[0])],
        flops=400_000,
        moved=1_200_000,
        name="column_sum",
    )
    p0, p1 = send_on(out, 0), send_on(out, 8)
    normed, kept = local_call(
        next_body,
        [("vmem", (PAIR, D), BF), ("vmem", (PIECE, D), BF)],
        [("smem", where)] + [("vmem", a) for a in (kept, p0, p1, factors[1])],
        flops=1_000_000,
        moved=800_000,
        name="norm_next",
    )
    kept = send_on(kept, 0)
    sums, kv, (cache,) = block(True, normed, kept, where, w1, w2, gains, kv)
    here, there = local_call(
        last_column_body,
        [("vmem", (PIECE, D), BF)] * 2,
        [("smem", where)] + [("vmem", a) for a in sums] + [("vmem", factors[1])],
        flops=400_000,
        moved=1_200_000,
        name="column_last",
    )
    p0, p1 = send_on(here, 0), send_on(there, 8)
    (out,) = local_call(
        final_body,
        [("hbm", (PIECE, D), BF)],
        [("vmem", a) for a in (kept, p0, p1)],
        flops=400_000,
        moved=400_000,
        name="residual_last",
    )
    return out[None], cache[None]


def solution(mesh):
    return jax.shard_map(
        shards,
        mesh=mesh,
        in_specs=(
            P("section", "sp", None),
            P(),
            P(),
            P("section", None, None, None),
            P("section", None, None, "sp"),
            P("section", None, None),
            P("section", None, "sp"),
            P("section", "sp", None),
            P("section", "sp", None),
            P("section", None, None, "sp"),
        ),
        out_specs=(P("section", "sp", None), P("section", None, None, "sp")),
        check_vma=False,
    )
```

```python
import functools
import math

import jax
import jax.numpy as jnp
from jax import lax
from jax.experimental import pallas as pl
from jax.experimental.pallas import tpu as pltpu
from jax.sharding import PartitionSpec as P

HD = 128
D = 3072
ROWS = 256
TOKENS = 4096
HIDDEN = 384
PIECE = 16
PAIR = 32
HALF = 128
SECTIONS = 16
SPAN = 16
BF = jnp.bfloat16
F32 = jnp.float32
MIB = 1 << 20
EXPONENT = 1.0 / (math.sqrt(HD) * math.log(2.0))


def send_core(x):
    return lax.ppermute(x, "sp", [(i, i ^ 1) for i in range(SPAN)])


def send_y(x, by):
    return lax.ppermute(
        x, "sp", [(i, (i & 9) | ((((i >> 1) & 3) + by) % 4) << 1) for i in range(SPAN)]
    )


def send_x(x):
    return lax.ppermute(x, "sp", [(i, i ^ 8) for i in range(SPAN)])


def send_on(x, flip):
    pairs = []
    for s in range(SECTIONS):
        for i in range(SPAN):
            pairs.append((s * SPAN + i, ((s + 1) % SECTIONS) * SPAN + (i ^ flip)))
    return lax.ppermute(x, ("section", "sp"), pairs)


def in_vmem(x):
    return pltpu.with_memory_space_constraint(x, pltpu.VMEM)


def local_call(body, outs, args, scratch=(), limit=16, flops=0, moved=0, name=None, aliases=None):
    specs = []
    given = []
    for kind, arg in args:
        if kind == "smem":
            specs.append(pl.BlockSpec(memory_space=pltpu.SMEM))
            given.append(arg)
        elif kind == "any":
            specs.append(pl.BlockSpec(memory_space=pl.ANY))
            given.append(arg)
        elif kind == "hbm":
            specs.append(pl.BlockSpec(memory_space=pltpu.HBM))
            given.append(pltpu.with_memory_space_constraint(arg, pltpu.HBM))
        else:
            specs.append(pl.BlockSpec(memory_space=pltpu.VMEM))
            given.append(in_vmem(arg))
    out_specs = []
    out_shape = []
    for kind, shape, dtype in outs:
        if kind in ("any", "hbm"):
            space = pl.ANY if kind == "any" else pltpu.VMEM
            out_specs.append(pl.BlockSpec(memory_space=space))
            out_shape.append(jax.ShapeDtypeStruct(shape, dtype))
        else:
            out_specs.append(pl.BlockSpec(memory_space=pltpu.VMEM))
            out_shape.append(pltpu.VMEM(shape, dtype))
    return pl.pallas_call(
        body,
        out_shape=out_shape,
        in_specs=specs,
        out_specs=out_specs,
        scratch_shapes=list(scratch),
        input_output_aliases=aliases or {},
        compiler_params=pltpu.CompilerParams(vmem_limit_bytes=limit * MIB),
        cost_estimate=pl.CostEstimate(flops=flops, bytes_accessed=moved, transcendentals=0),
        name=name,
    )(*given)


def layer_norm(wide, factors):
    center = wide - jnp.mean(wide, axis=-1, keepdims=True)
    spread = jnp.mean(center * center, axis=-1, keepdims=True)
    shift = factors[0:1, :]
    scale = factors[1:2, :]
    return (center * lax.rsqrt(spread + 1e-06) * (1.0 + scale) + shift).astype(BF)


def spot():
    place = lax.axis_index("sp")
    return lax.div(place, 8), lax.rem(lax.div(place, 2), 4), lax.rem(place, 2)


def turn(round_id):
    section = lax.axis_index("section")
    anchor = lax.rem(section - round_id + SECTIONS, SECTIONS)
    return anchor, jnp.where(section < round_id, 1, 0)


def start_body(own, other, factors, normed, kept):
    xh, _, _ = spot()
    mine = pl.multiple_of(xh * PIECE, PIECE)
    theirs = pl.multiple_of((1 - xh) * PIECE, PIECE)
    kept[pl.ds(mine, PIECE), :] = own[...]
    kept[pl.ds(theirs, PIECE), :] = other[...]
    table = factors[...]
    normed[pl.ds(mine, PIECE), :] = layer_norm(own[...].astype(F32), table)
    normed[pl.ds(theirs, PIECE), :] = layer_norm(other[...].astype(F32), table)


def fetch_body(steps, modulation, w_qkv, w_mlp_in, cache, w1, first, second, kv, table, sems):
    pairs = [(modulation, table)]
    pairs += [(w_qkv.at[i], w1.at[:, i * HD:(i + 1) * HD]) for i in range(3)]
    pairs += [(w_mlp_in, w1.at[:, 3 * HD:])]
    pairs += [(cache.at[i], kv.at[i]) for i in range(2)]
    copies = [pltpu.make_async_copy(a, b, sems.at[i]) for i, (a, b) in enumerate(pairs)]
    for c in copies:
        c.start()
    copies[0].wait()
    for round_id, out in ((0, first), (1, second)):
        anchor, late = turn(round_id)
        step = steps[anchor] + late
        for k in range(3):
            plane = table[k].astype(F32)
            hit = lax.broadcasted_iota(jnp.int32, plane.shape, 0) == step
            out[k:k + 1, :] = jnp.sum(jnp.where(hit, plane, 0.0), axis=0, keepdims=True)
    for c in copies[1:]:
        c.wait()


def head_norm(part, gain):
    wide = part.astype(F32)
    power = jnp.mean(wide * wide, axis=-1, keepdims=True)
    return (wide * lax.rsqrt(power + 1e-06) * gain.astype(F32)).astype(BF)


def gelu(x):
    return jax.nn.gelu(x, approximate=True)


def attend(query, kv, scores):
    rows = query.shape[0]
    step = 512
    top = None
    for j in range(TOKENS // step):
        s = lax.dot_general(
            query, kv[0, j * step:(j + 1) * step, :], (((1,), (1,)), ((), ())),
            preferred_element_type=F32,
        )
        scores[0:rows, j * step:(j + 1) * step] = s
        best = jnp.max(s, axis=-1, keepdims=True)
        top = best if top is None else jnp.maximum(top, best)
    total = None
    mixed = None
    for j in range(TOKENS // step):
        e = jnp.exp2((scores[0:rows, j * step:(j + 1) * step] - top) * EXPONENT)
        t = jnp.sum(e, axis=-1, keepdims=True)
        m = jnp.dot(
            e.astype(BF), kv[1, j * step:(j + 1) * step, :], preferred_element_type=F32
        )
        total = t if total is None else total + t
        mixed = m if mixed is None else mixed + m
    return (mixed / total).astype(BF)


def block_body(last, patches, n0, n3, n1, n2, s0, s3, s1, s2, w1, gains, *rest):
    if last:
        (old, w2, kv, joined, queries, partial, new_cache, rows, scores, sems) = rest
        reads = []
    else:
        (old, w_attn_out, w_mlp_out, kv, joined, queries, partial, w2, rows, scores, sems) = rest
        pairs = [(w_attn_out, w2.at[:HD, :]), (w_mlp_out, w2.at[HD:, :])]
        reads = [pltpu.make_async_copy(a, b, sems.at[i]) for i, (a, b) in enumerate(pairs)]
    for r in reads:
        r.start()
    anchor, _ = turn(1 if last else 0)
    patch = pl.multiple_of(patches[anchor] * ROWS, ROWS)
    _, y, core = spot()
    for i, piece in enumerate((n0, n1, n2, n3, s0, s1, s2, s3)):
        rows[i * PAIR:(i + 1) * PAIR, :] = piece[...]
    h = rows[...]
    qk = jnp.dot(h, w1[:, 0:256], preferred_element_type=F32).astype(BF)
    vm = jnp.dot(h, w1[:, 256:512], preferred_element_type=F32)
    mm = jnp.dot(h, w1[:, 512:768], preferred_element_type=F32)
    query = head_norm(qk[:, :HD], gains[0:1, :])
    key = head_norm(qk[:, HD:], gains[1:2, :])
    value = vm[:, :HD].astype(BF)
    joined[:, HD:2 * HD] = gelu(vm[:, HD:]).astype(BF)
    joined[:, 2 * HD:] = gelu(mm).astype(BF)
    for dc in range(2):
        for dy in range(4):
            for x in range(2):
                at = (dc * 4 + dy) * PAIR + x * PIECE
                row = x * HALF + lax.rem(y + dy, 4) * PAIR + jnp.where(core == dc, 0, PIECE)
                to = pl.multiple_of(patch + row, PIECE)
                kv[0, pl.ds(to, PIECE), :] = key[at:at + PIECE, :]
                kv[1, pl.ds(to, PIECE), :] = value[at:at + PIECE, :]
    writes = []
    if last:
        writes = [pltpu.make_async_copy(kv.at[i], new_cache.at[i], sems.at[i]) for i in range(2)]
    for w in writes:
        w.start()
    queries[...] = query[:HALF, :]
    joined[HALF:, 0:HD] = attend(query[HALF:, :], kv, scores)
    for r in reads:
        r.wait()
    theirs = joined[HALF:, :]
    for j in range(D // 256):
        partial[:, j * 256:(j + 1) * 256] = jnp.dot(
            theirs, w2[:, j * 256:(j + 1) * 256], preferred_element_type=F32
        ).astype(BF)
    for w in writes:
        w.wait()


def own_body(queries, kv, joined, w2, partial, scores):
    mixed = attend(queries[...], kv, scores)
    mine = jnp.concatenate([mixed, joined[:HALF, HD:]], axis=1)
    for j in range(D // 256):
        partial[:, j * 256:(j + 1) * 256] = jnp.dot(
            mine, w2[:, j * 256:(j + 1) * 256], preferred_element_type=F32
        )


def pair_body(mine, came, o0, o1, o2, o3):
    o0[...] = mine[0:PAIR, :] + came[0:PAIR, :].astype(F32)
    for i, o in ((1, o1), (2, o2), (3, o3)):
        a, b = i * PAIR, (i + 1) * PAIR
        o[...] = (mine[a:b, :] + came[a:b, :].astype(F32)).astype(BF)


def column_body(mine, r2, r3, r1, factors, out):
    total = mine[...] + r1[...].astype(F32) + (r2[...].astype(F32) + r3[...].astype(F32))
    out[...] = (factors[2:3, :] * total).astype(BF)


def last_column_body(mine, r2, r3, r1, factors, here, there):
    xh, _, _ = spot()
    gate = factors[2:3, :]
    for out, at in ((here, xh), (there, 1 - xh)):
        rows = pl.ds(pl.multiple_of(at * PIECE, PIECE), PIECE)
        total = mine[rows, :] + r1[rows, :].astype(F32)
        total = total + (r2[rows, :].astype(F32) + r3[rows, :].astype(F32))
        out[...] = (gate * total).astype(BF)


def next_body(kept, p0, p1, factors, normed, own):
    xh, _, _ = spot()
    new = (kept[...].astype(F32) + (p0[...].astype(F32) + p1[...].astype(F32))).astype(BF)
    wide = new.astype(F32)
    normed[...] = layer_norm(wide, factors[...])
    own[...] = jnp.where(xh == 0, new[:PIECE, :], new[PIECE:, :])


def final_body(kept, p0, p1, out):
    out[...] = (kept[...].astype(F32) + (p0[...].astype(F32) + p1[...].astype(F32))).astype(BF)


def block(last, normed, patches, w1, gains, kv, weights):
    core_parts = [send_core(normed)]
    n2 = send_y(normed, 2)
    n3 = send_y(normed, 1)
    n1 = send_y(normed, 3)
    core_parts += [send_core(p) for p in (n3, n1, n2)]
    cache_shape = (2, TOKENS, HD)
    outs = [
        ("vmem", cache_shape, BF),
        ("vmem", (ROWS, 4 * HD), BF),
        ("vmem", (HALF, HD), BF),
        ("vmem", (HALF, D), BF),
    ]
    outs.append(("any", cache_shape, BF) if last else ("vmem", (4 * HD, D), BF))
    kind = "vmem" if last else "hbm"
    kv, joined, queries, partial, fifth = local_call(
        functools.partial(block_body, last),
        outs,
        [("smem", patches)] + [("vmem", p) for p in [normed, n3, n1, n2] + core_parts]
        + [("vmem", w1), ("vmem", gains), ("vmem", kv)] + [(kind, a) for a in weights],
        scratch=[
            pltpu.VMEM((ROWS, D), BF),
            pltpu.VMEM((HALF, TOKENS), F32),
            pltpu.SemaphoreType.DMA((2,)),
        ],
        limit=24,
        flops=2_200_000_000,
        moved=12_000_000,
        name="block",
        aliases={11: 0},
    )
    w2 = weights[0] if last else fifth
    came = send_core(partial)
    (mine,) = local_call(
        own_body,
        [("vmem", (HALF, D), F32)],
        [("vmem", queries), ("vmem", kv), ("vmem", joined), ("vmem", w2)],
        scratch=[pltpu.VMEM((HALF, TOKENS), F32)],
        flops=700_000_000,
        moved=4_700_000,
        name="own_half",
    )
    o0, o1, o2, o3 = local_call(
        pair_body,
        [("vmem", (PAIR, D), F32)] + [("vmem", (PAIR, D), BF)] * 3,
        [("vmem", mine), ("vmem", came)],
        flops=400_000,
        moved=3_000_000,
        name="pair_sum",
    )
    r2 = send_y(o2, 2)
    r1 = send_y(o1, 1)
    r3 = send_y(o3, 3)
    return (o0, r2, r3, r1), kv, fifth


def shards(
    slots,
    patch_of_slot,
    step_of_slot,
    modulation,
    w_qkv,
    qk_scale,
    w_mlp_in,
    w_attn_out,
    w_mlp_out,
    kv_cache,
):
    own = slots[0]
    other = send_x(own)
    gains = qk_scale[0]
    w1, first, second, kv = local_call(
        fetch_body,
        [
            ("vmem", (D, 6 * HD), BF),
            ("vmem", (3, D), F32),
            ("vmem", (3, D), F32),
            ("vmem", (2, TOKENS, HD), BF),
        ],
        [
            ("smem", step_of_slot),
            ("hbm", jnp.transpose(modulation[0], (1, 0, 2))),
            ("hbm", jnp.transpose(w_qkv[0], (1, 0, 2))),
            ("hbm", w_mlp_in[0]),
            ("hbm", kv_cache[0]),
        ],
        scratch=[pltpu.VMEM((3, modulation.shape[1], D), BF), pltpu.SemaphoreType.DMA((7,))],
        flops=0,
        moved=7_000_000,
        name="fetch",
    )
    factors = (first, second)

    normed, kept = local_call(
        start_body,
        [("vmem", (PAIR, D), BF)] * 2,
        [("vmem", own), ("vmem", other), ("vmem", factors[0])],
        flops=1_000_000,
        moved=400_000,
        name="norm_first",
    )
    kept = send_on(kept, 0)
    sums, kv, w2 = block(
        False, normed, patch_of_slot, w1, gains, kv, (w_attn_out[0], w_mlp_out[0])
    )
    (out,) = local_call(
        column_body,
        [("vmem", (PAIR, D), BF)],
        [("vmem", a) for a in sums] + [("vmem", factors[0])],
        flops=400_000,
        moved=1_200_000,
        name="column_sum",
    )
    p0, p1 = send_on(out, 0), send_on(out, 8)
    normed, kept = local_call(
        next_body,
        [("vmem", (PAIR, D), BF), ("vmem", (PIECE, D), BF)],
        [("vmem", a) for a in (kept, p0, p1, factors[1])],
        flops=1_000_000,
        moved=800_000,
        name="norm_next",
    )
    kept = send_on(kept, 0)
    sums, _, cache = block(True, normed, patch_of_slot, w1, gains, kv, (w2,))
    here, there = local_call(
        last_column_body,
        [("vmem", (PIECE, D), BF)] * 2,
        [("vmem", a) for a in sums] + [("vmem", factors[1])],
        flops=400_000,
        moved=1_200_000,
        name="column_last",
    )
    p0, p1 = send_on(here, 0), send_on(there, 8)
    (out,) = local_call(
        final_body,
        [("hbm", (PIECE, D), BF)],
        [("vmem", a) for a in (kept, p0, p1)],
        flops=400_000,
        moved=400_000,
        name="residual_last",
    )
    return out[None], cache[None]


def solution(mesh):
    return jax.shard_map(
        shards,
        mesh=mesh,
        in_specs=(
            P("section", "sp", None),
            P(),
            P(),
            P("section", None, None, None),
            P("section", None, None, "sp"),
            P("section", None, None),
            P("section", None, "sp"),
            P("section", "sp", None),
            P("section", "sp", None),
            P("section", None, None, "sp"),
        ),
        out_specs=(P("section", "sp", None), P("section", None, None, "sp")),
        check_vma=False,
    )
```

```python
import functools
import math

import jax
import jax.numpy as jnp
from jax import lax
from jax.experimental import pallas as pl
from jax.experimental.pallas import tpu as pltpu
from jax.sharding import PartitionSpec as P

HD = 128
D = 3072
ROWS = 256
TOKENS = 4096
HIDDEN = 384
PIECE = 16
PAIR = 32
HALF = 128
SECTIONS = 16
SPAN = 16
BF = jnp.bfloat16
F32 = jnp.float32
MIB = 1 << 20
EXPONENT = 1.0 / (math.sqrt(HD) * math.log(2.0))


def send_core(x):
    return lax.ppermute(x, "sp", [(i, i ^ 1) for i in range(SPAN)])


def send_y(x, by):
    return lax.ppermute(
        x, "sp", [(i, (i & 9) | ((((i >> 1) & 3) + by) % 4) << 1) for i in range(SPAN)]
    )


def send_x(x):
    return lax.ppermute(x, "sp", [(i, i ^ 8) for i in range(SPAN)])


def send_on(x, flip):
    pairs = []
    for s in range(SECTIONS):
        for i in range(SPAN):
            pairs.append((s * SPAN + i, ((s + 1) % SECTIONS) * SPAN + (i ^ flip)))
    return lax.ppermute(x, ("section", "sp"), pairs)


def in_vmem(x):
    return pltpu.with_memory_space_constraint(x, pltpu.VMEM)


def local_call(body, outs, args, scratch=(), limit=16, flops=0, moved=0, name=None, aliases=None):
    specs = []
    given = []
    for kind, arg in args:
        if kind == "smem":
            specs.append(pl.BlockSpec(memory_space=pltpu.SMEM))
            given.append(arg)
        elif kind == "any":
            specs.append(pl.BlockSpec(memory_space=pl.ANY))
            given.append(arg)
        elif kind == "hbm":
            specs.append(pl.BlockSpec(memory_space=pltpu.HBM))
            given.append(pltpu.with_memory_space_constraint(arg, pltpu.HBM))
        else:
            specs.append(pl.BlockSpec(memory_space=pltpu.VMEM))
            given.append(in_vmem(arg))
    out_specs = []
    out_shape = []
    for kind, shape, dtype in outs:
        if kind in ("any", "hbm"):
            space = pl.ANY if kind == "any" else pltpu.VMEM
            out_specs.append(pl.BlockSpec(memory_space=space))
            out_shape.append(jax.ShapeDtypeStruct(shape, dtype))
        else:
            out_specs.append(pl.BlockSpec(memory_space=pltpu.VMEM))
            out_shape.append(pltpu.VMEM(shape, dtype))
    return pl.pallas_call(
        body,
        out_shape=out_shape,
        in_specs=specs,
        out_specs=out_specs,
        scratch_shapes=list(scratch),
        input_output_aliases=aliases or {},
        compiler_params=pltpu.CompilerParams(vmem_limit_bytes=limit * MIB),
        cost_estimate=pl.CostEstimate(flops=flops, bytes_accessed=moved, transcendentals=0),
        name=name,
    )(*given)


def layer_norm(wide, factors):
    center = wide - jnp.mean(wide, axis=-1, keepdims=True)
    spread = jnp.mean(center * center, axis=-1, keepdims=True)
    shift = factors[0:1, :]
    scale = factors[1:2, :]
    return (center * lax.rsqrt(spread + 1e-06) * (1.0 + scale) + shift).astype(BF)


def spot():
    place = lax.axis_index("sp")
    return lax.div(place, 8), lax.rem(lax.div(place, 2), 4), lax.rem(place, 2)


def turn(round_id):
    section = lax.axis_index("section")
    anchor = lax.rem(section - round_id + SECTIONS, SECTIONS)
    return anchor, jnp.where(section < round_id, 1, 0)


def start_body(own, other, factors, normed, kept):
    xh, _, _ = spot()
    mine = pl.multiple_of(xh * PIECE, PIECE)
    theirs = pl.multiple_of((1 - xh) * PIECE, PIECE)
    kept[pl.ds(mine, PIECE), :] = own[...]
    kept[pl.ds(theirs, PIECE), :] = other[...]
    table = factors[...]
    normed[pl.ds(mine, PIECE), :] = layer_norm(own[...].astype(F32), table)
    normed[pl.ds(theirs, PIECE), :] = layer_norm(other[...].astype(F32), table)


def fetch_body(steps, modulation, w_qkv, w_mlp_in, cache, w1, first, second, kv, table, sems):
    pairs = [(modulation, table)]
    pairs += [(w_qkv.at[i], w1.at[:, i * HD:(i + 1) * HD]) for i in range(3)]
    pairs += [(w_mlp_in, w1.at[:, 3 * HD:])]
    pairs += [(cache.at[i], kv.at[i]) for i in range(2)]
    copies = [pltpu.make_async_copy(a, b, sems.at[i]) for i, (a, b) in enumerate(pairs)]
    for c in copies:
        c.start()
    copies[0].wait()
    for round_id, out in ((0, first), (1, second)):
        anchor, late = turn(round_id)
        step = steps[anchor] + late
        for k in range(3):
            plane = table[k].astype(F32)
            hit = lax.broadcasted_iota(jnp.int32, plane.shape, 0) == step
            out[k:k + 1, :] = jnp.sum(jnp.where(hit, plane, 0.0), axis=0, keepdims=True)
    for c in copies[1:]:
        c.wait()


def head_norm(part, gain):
    wide = part.astype(F32)
    power = jnp.mean(wide * wide, axis=-1, keepdims=True)
    return (wide * lax.rsqrt(power + 1e-06) * gain.astype(F32)).astype(BF)


def gelu(x):
    return jax.nn.gelu(x, approximate=True)


def attend(query, kv, scores):
    rows = query.shape[0]
    step = 512
    top = None
    for j in range(TOKENS // step):
        s = lax.dot_general(
            query, kv[0, j * step:(j + 1) * step, :], (((1,), (1,)), ((), ())),
            preferred_element_type=F32,
        )
        scores[0:rows, j * step:(j + 1) * step] = s
        best = jnp.max(s, axis=-1, keepdims=True)
        top = best if top is None else jnp.maximum(top, best)
    total = None
    mixed = None
    for j in range(TOKENS // step):
        e = jnp.exp2((scores[0:rows, j * step:(j + 1) * step] - top) * EXPONENT)
        t = jnp.sum(e, axis=-1, keepdims=True)
        m = jnp.dot(
            e.astype(BF), kv[1, j * step:(j + 1) * step, :], preferred_element_type=F32
        )
        total = t if total is None else total + t
        mixed = m if mixed is None else mixed + m
    return (mixed / total).astype(BF)


def block_body(last, patches, n0, n2, n1, n3, s0, s2, s1, s3, w1, gains, *rest):
    if last:
        (old, w2, kv, joined, queries, partial, new_cache, rows, scores, sems) = rest
        reads = []
    else:
        (old, w_attn_out, w_mlp_out, kv, joined, queries, partial, w2, rows, scores, sems) = rest
        pairs = [(w_attn_out, w2.at[:HD, :]), (w_mlp_out, w2.at[HD:, :])]
        reads = [pltpu.make_async_copy(a, b, sems.at[i]) for i, (a, b) in enumerate(pairs)]
    for r in reads:
        r.start()
    anchor, _ = turn(1 if last else 0)
    patch = pl.multiple_of(patches[anchor] * ROWS, ROWS)
    _, y, core = spot()
    for i, piece in enumerate((n0, n1, n2, n3, s0, s1, s2, s3)):
        rows[i * PAIR:(i + 1) * PAIR, :] = piece[...]
    h = rows[...]
    qk = jnp.dot(h, w1[:, 0:256], preferred_element_type=F32).astype(BF)
    vm = jnp.dot(h, w1[:, 256:512], preferred_element_type=F32)
    mm = jnp.dot(h, w1[:, 512:768], preferred_element_type=F32)
    query = head_norm(qk[:, :HD], gains[0:1, :])
    key = head_norm(qk[:, HD:], gains[1:2, :])
    value = vm[:, :HD].astype(BF)
    joined[:, HD:2 * HD] = gelu(vm[:, HD:]).astype(BF)
    joined[:, 2 * HD:] = gelu(mm).astype(BF)
    for dc in range(2):
        for dy in range(4):
            for x in range(2):
                at = (dc * 4 + dy) * PAIR + x * PIECE
                row = x * HALF + lax.rem(y + dy, 4) * PAIR + jnp.where(core == dc, 0, PIECE)
                to = pl.multiple_of(patch + row, PIECE)
                kv[0, pl.ds(to, PIECE), :] = key[at:at + PIECE, :]
                kv[1, pl.ds(to, PIECE), :] = value[at:at + PIECE, :]
    writes = []
    if last:
        writes = [pltpu.make_async_copy(kv.at[i], new_cache.at[i], sems.at[i]) for i in range(2)]
    for w in writes:
        w.start()
    queries[...] = query[:HALF, :]
    joined[HALF:, 0:HD] = attend(query[HALF:, :], kv, scores)
    for r in reads:
        r.wait()
    theirs = joined[HALF:, :]
    for j in range(D // 256):
        partial[:, j * 256:(j + 1) * 256] = jnp.dot(
            theirs, w2[:, j * 256:(j + 1) * 256], preferred_element_type=F32
        ).astype(BF)
    for w in writes:
        w.wait()


def own_body(queries, kv, joined, w2, partial, scores):
    mixed = attend(queries[...], kv, scores)
    mine = jnp.concatenate([mixed, joined[:HALF, HD:]], axis=1)
    for j in range(D // 256):
        partial[:, j * 256:(j + 1) * 256] = jnp.dot(
            mine, w2[:, j * 256:(j + 1) * 256], preferred_element_type=F32
        )


def pair_body(mine, came, passing, o0, o1, o2, o3):
    o0[...] = mine[0:PAIR, :] + came[0:PAIR, :].astype(F32)
    for i, o in ((1, o1), (2, o2), (3, o3)):
        a, b = i * PAIR, (i + 1) * PAIR
        o[...] = (mine[a:b, :] + came[a:b, :].astype(F32)).astype(BF)


def column_body(mine, r1, r3, r2, factors, out):
    total = mine[...] + r1[...].astype(F32) + (r2[...].astype(F32) + r3[...].astype(F32))
    out[...] = (factors[2:3, :] * total).astype(BF)


def last_column_body(mine, r1, r3, r2, factors, here, there):
    xh, _, _ = spot()
    gate = factors[2:3, :]
    for out, at in ((here, xh), (there, 1 - xh)):
        rows = pl.ds(pl.multiple_of(at * PIECE, PIECE), PIECE)
        total = mine[rows, :] + r1[rows, :].astype(F32)
        total = total + (r2[rows, :].astype(F32) + r3[rows, :].astype(F32))
        out[...] = (gate * total).astype(BF)


def next_body(kept, p0, p1, factors, normed, own):
    xh, _, _ = spot()
    new = (kept[...].astype(F32) + (p0[...].astype(F32) + p1[...].astype(F32))).astype(BF)
    wide = new.astype(F32)
    normed[...] = layer_norm(wide, factors[...])
    own[...] = jnp.where(xh == 0, new[:PIECE, :], new[PIECE:, :])


def final_body(kept, p0, p1, out):
    out[...] = (kept[...].astype(F32) + (p0[...].astype(F32) + p1[...].astype(F32))).astype(BF)


def block(last, normed, passing, patches, w1, gains, kv, weights):
    core_parts = [send_core(normed)]
    n2 = send_y(normed, 2)
    n3 = send_y(normed, 1)
    n1 = send_y(normed, 3)
    core_parts += [send_core(p) for p in (n2, n1, n3)]
    cache_shape = (2, TOKENS, HD)
    outs = [
        ("vmem", cache_shape, BF),
        ("vmem", (ROWS, 4 * HD), BF),
        ("vmem", (HALF, HD), BF),
        ("vmem", (HALF, D), BF),
    ]
    outs.append(("any", cache_shape, BF) if last else ("vmem", (4 * HD, D), BF))
    kind = "vmem" if last else "hbm"
    kv, joined, queries, partial, fifth = local_call(
        functools.partial(block_body, last),
        outs,
        [("smem", patches)] + [("vmem", p) for p in [normed, n2, n1, n3] + core_parts]
        + [("vmem", w1), ("vmem", gains), ("vmem", kv)] + [(kind, a) for a in weights],
        scratch=[
            pltpu.VMEM((ROWS, D), BF),
            pltpu.VMEM((HALF, TOKENS), F32),
            pltpu.SemaphoreType.DMA((2,)),
        ],
        limit=24,
        flops=30_000_000_000,
        moved=12_000_000,
        name="block",
        aliases={11: 0},
    )
    w2 = weights[0] if last else fifth
    came = send_core(partial)
    (mine,) = local_call(
        own_body,
        [("vmem", (HALF, D), F32)],
        [("vmem", queries), ("vmem", kv), ("vmem", joined), ("vmem", w2)],
        scratch=[pltpu.VMEM((HALF, TOKENS), F32)],
        flops=12_000_000_000,
        moved=4_700_000,
        name="own_half",
    )
    o0, o1, o2, o3 = local_call(
        pair_body,
        [("vmem", (PAIR, D), F32)] + [("vmem", (PAIR, D), BF)] * 3,
        [("vmem", mine), ("vmem", came), ("any", passing)],
        flops=400_000,
        moved=3_000_000,
        name="pair_sum",
    )
    r2 = send_y(o2, 2)
    r1 = send_y(o1, 1)
    r3 = send_y(o3, 3)
    return (o0, r1, r3, r2), kv, fifth


def shards(
    slots,
    patch_of_slot,
    step_of_slot,
    modulation,
    w_qkv,
    qk_scale,
    w_mlp_in,
    w_attn_out,
    w_mlp_out,
    kv_cache,
):
    own = slots[0]
    other = send_x(own)
    gains = qk_scale[0]
    w1, first, second, kv = local_call(
        fetch_body,
        [
            ("vmem", (D, 6 * HD), BF),
            ("vmem", (3, D), F32),
            ("vmem", (3, D), F32),
            ("vmem", (2, TOKENS, HD), BF),
        ],
        [
            ("smem", step_of_slot),
            ("hbm", jnp.transpose(modulation[0], (1, 0, 2))),
            ("hbm", jnp.transpose(w_qkv[0], (1, 0, 2))),
            ("hbm", w_mlp_in[0]),
            ("hbm", kv_cache[0]),
        ],
        scratch=[pltpu.VMEM((3, modulation.shape[1], D), BF), pltpu.SemaphoreType.DMA((7,))],
        flops=0,
        moved=7_000_000,
        name="fetch",
    )
    factors = (first, second)

    normed, kept = local_call(
        start_body,
        [("vmem", (PAIR, D), BF)] * 2,
        [("vmem", own), ("vmem", other), ("vmem", factors[0])],
        flops=1_000_000,
        moved=400_000,
        name="norm_first",
    )
    kept = send_on(kept, 0)
    sums, kv, w2 = block(
        False, normed, kept, patch_of_slot, w1, gains, kv, (w_attn_out[0], w_mlp_out[0])
    )
    (out,) = local_call(
        column_body,
        [("vmem", (PAIR, D), BF)],
        [("vmem", a) for a in sums] + [("vmem", factors[0])],
        flops=400_000,
        moved=1_200_000,
        name="column_sum",
    )
    p0, p1 = send_on(out, 0), send_on(out, 8)
    normed, kept = local_call(
        next_body,
        [("vmem", (PAIR, D), BF), ("vmem", (PIECE, D), BF)],
        [("vmem", a) for a in (kept, p0, p1, factors[1])],
        flops=1_000_000,
        moved=800_000,
        name="norm_next",
    )
    kept = send_on(kept, 0)
    sums, _, cache = block(True, normed, kept, patch_of_slot, w1, gains, kv, (w2,))
    here, there = local_call(
        last_column_body,
        [("vmem", (PIECE, D), BF)] * 2,
        [("vmem", a) for a in sums] + [("vmem", factors[1])],
        flops=400_000,
        moved=1_200_000,
        name="column_last",
    )
    p0, p1 = send_on(here, 0), send_on(there, 8)
    (out,) = local_call(
        final_body,
        [("hbm", (PIECE, D), BF)],
        [("vmem", a) for a in (kept, p0, p1)],
        flops=400_000,
        moved=400_000,
        name="residual_last",
    )
    return out[None], cache[None]


def solution(mesh):
    return jax.shard_map(
        shards,
        mesh=mesh,
        in_specs=(
            P("section", "sp", None),
            P(),
            P(),
            P("section", None, None, None),
            P("section", None, None, "sp"),
            P("section", None, None),
            P("section", None, "sp"),
            P("section", "sp", None),
            P("section", "sp", None),
            P("section", None, None, "sp"),
        ),
        out_specs=(P("section", "sp", None), P("section", None, None, "sp")),
        check_vma=False,
    )
```

```python
import functools
import math

import jax
import jax.numpy as jnp
from jax import lax
from jax.experimental import pallas as pl
from jax.experimental.pallas import tpu as pltpu
from jax.sharding import PartitionSpec as P

HD = 128
D = 3072
ROWS = 256
TOKENS = 4096
HIDDEN = 384
PIECE = 16
PAIR = 32
HALF = 128
SECTIONS = 16
SPAN = 16
BF = jnp.bfloat16
F32 = jnp.float32
MIB = 1 << 20
EXPONENT = 1.0 / (math.sqrt(HD) * math.log(2.0))


def send_core(x):
    return lax.ppermute(x, "sp", [(i, i ^ 1) for i in range(SPAN)])


def send_y(x, by):
    return lax.ppermute(
        x, "sp", [(i, (i & 9) | ((((i >> 1) & 3) + by) % 4) << 1) for i in range(SPAN)]
    )


def send_x(x):
    return lax.ppermute(x, "sp", [(i, i ^ 8) for i in range(SPAN)])


def send_on(x, flip):
    pairs = []
    for s in range(SECTIONS):
        for i in range(SPAN):
            pairs.append((s * SPAN + i, ((s + 1) % SECTIONS) * SPAN + (i ^ flip)))
    return lax.ppermute(x, ("section", "sp"), pairs)


def in_vmem(x):
    return pltpu.with_memory_space_constraint(x, pltpu.VMEM)


def local_call(body, outs, args, scratch=(), limit=16, flops=0, moved=0, name=None, aliases=None):
    specs = []
    given = []
    for kind, arg in args:
        if kind == "smem":
            specs.append(pl.BlockSpec(memory_space=pltpu.SMEM))
            given.append(arg)
        elif kind == "any":
            specs.append(pl.BlockSpec(memory_space=pl.ANY))
            given.append(arg)
        elif kind == "hbm":
            specs.append(pl.BlockSpec(memory_space=pltpu.HBM))
            given.append(pltpu.with_memory_space_constraint(arg, pltpu.HBM))
        else:
            specs.append(pl.BlockSpec(memory_space=pltpu.VMEM))
            given.append(in_vmem(arg))
    out_specs = []
    out_shape = []
    for kind, shape, dtype in outs:
        if kind in ("any", "hbm"):
            space = pl.ANY if kind == "any" else pltpu.VMEM
            out_specs.append(pl.BlockSpec(memory_space=space))
            out_shape.append(jax.ShapeDtypeStruct(shape, dtype))
        else:
            out_specs.append(pl.BlockSpec(memory_space=pltpu.VMEM))
            out_shape.append(pltpu.VMEM(shape, dtype))
    return pl.pallas_call(
        body,
        out_shape=out_shape,
        in_specs=specs,
        out_specs=out_specs,
        scratch_shapes=list(scratch),
        input_output_aliases=aliases or {},
        compiler_params=pltpu.CompilerParams(vmem_limit_bytes=limit * MIB),
        cost_estimate=pl.CostEstimate(flops=flops, bytes_accessed=moved, transcendentals=0),
        name=name,
    )(*given)


def layer_norm(wide, factors):
    center = wide - jnp.mean(wide, axis=-1, keepdims=True)
    spread = jnp.mean(center * center, axis=-1, keepdims=True)
    shift = factors[0:1, :]
    scale = factors[1:2, :]
    return (center * lax.rsqrt(spread + 1e-06) * (1.0 + scale) + shift).astype(BF)


def spot():
    place = lax.axis_index("sp")
    return lax.div(place, 8), lax.rem(lax.div(place, 2), 4), lax.rem(place, 2)


def turn(round_id):
    section = lax.axis_index("section")
    anchor = lax.rem(section - round_id + SECTIONS, SECTIONS)
    return anchor, jnp.where(section < round_id, 1, 0)


def start_body(own, other, factors, normed, kept):
    xh, _, _ = spot()
    mine = pl.multiple_of(xh * PIECE, PIECE)
    theirs = pl.multiple_of((1 - xh) * PIECE, PIECE)
    kept[pl.ds(mine, PIECE), :] = own[...]
    kept[pl.ds(theirs, PIECE), :] = other[...]
    table = factors[...]
    normed[pl.ds(mine, PIECE), :] = layer_norm(own[...].astype(F32), table)
    normed[pl.ds(theirs, PIECE), :] = layer_norm(other[...].astype(F32), table)


def fetch_body(steps, modulation, w_qkv, w_mlp_in, cache, w1, first, second, kv, table, sems):
    pairs = [(modulation, table)]
    pairs += [(w_qkv.at[i], w1.at[:, i * HD:(i + 1) * HD]) for i in range(3)]
    pairs += [(w_mlp_in, w1.at[:, 3 * HD:])]
    pairs += [(cache.at[i], kv.at[i]) for i in range(2)]
    copies = [pltpu.make_async_copy(a, b, sems.at[i]) for i, (a, b) in enumerate(pairs)]
    for c in copies:
        c.start()
    copies[0].wait()
    for round_id, out in ((0, first), (1, second)):
        anchor, late = turn(round_id)
        step = steps[anchor] + late
        for k in range(3):
            plane = table[k].astype(F32)
            hit = lax.broadcasted_iota(jnp.int32, plane.shape, 0) == step
            out[k:k + 1, :] = jnp.sum(jnp.where(hit, plane, 0.0), axis=0, keepdims=True)
    for c in copies[1:]:
        c.wait()


def head_norm(part, gain):
    wide = part.astype(F32)
    power = jnp.mean(wide * wide, axis=-1, keepdims=True)
    return (wide * lax.rsqrt(power + 1e-06) * gain.astype(F32)).astype(BF)


def gelu(x):
    return jax.nn.gelu(x, approximate=True)


def attend(query, kv, scores):
    rows = query.shape[0]
    step = 512
    top = None
    for j in range(TOKENS // step):
        s = lax.dot_general(
            query, kv[0, j * step:(j + 1) * step, :], (((1,), (1,)), ((), ())),
            preferred_element_type=F32,
        )
        scores[0:rows, j * step:(j + 1) * step] = s
        best = jnp.max(s, axis=-1, keepdims=True)
        top = best if top is None else jnp.maximum(top, best)
    total = None
    mixed = None
    for j in range(TOKENS // step):
        e = jnp.exp2((scores[0:rows, j * step:(j + 1) * step] - top) * EXPONENT)
        t = jnp.sum(e, axis=-1, keepdims=True)
        m = jnp.dot(
            e.astype(BF), kv[1, j * step:(j + 1) * step, :], preferred_element_type=F32
        )
        total = t if total is None else total + t
        mixed = m if mixed is None else mixed + m
    return (mixed / total).astype(BF)


def project_body(n0, n2, n1, n3, w1, out, rows):
    for i, piece in enumerate((n0, n1, n2, n3)):
        rows[i * PAIR:(i + 1) * PAIR, :] = piece[...]
    for j in range(3):
        at = slice(j * 256, (j + 1) * 256)
        out[:, at] = jnp.dot(rows[...], w1[:, at], preferred_element_type=F32)


def block_body(last, patches, first, s0, s2, s1, s3, w1, gains, *rest):
    if last:
        (old, w2, kv, joined, queries, partial, new_cache, rows, scores, sems) = rest
        reads = []
    else:
        (old, w_attn_out, w_mlp_out, kv, joined, queries, partial, w2, rows, scores, sems) = rest
        pairs = [(w_attn_out, w2.at[:HD, :]), (w_mlp_out, w2.at[HD:, :])]
        reads = [pltpu.make_async_copy(a, b, sems.at[i]) for i, (a, b) in enumerate(pairs)]
    for r in reads:
        r.start()
    anchor, _ = turn(1 if last else 0)
    patch = pl.multiple_of(patches[anchor] * ROWS, ROWS)
    _, y, core = spot()
    for i, piece in enumerate((s0, s1, s2, s3)):
        rows[i * PAIR:(i + 1) * PAIR, :] = piece[...]
    parts = []
    for j in range(3):
        at = slice(j * 256, (j + 1) * 256)
        second = jnp.dot(rows[...], w1[:, at], preferred_element_type=F32)
        parts.append(jnp.concatenate([first[:, at], second], axis=0))
    qk, vm, mm = parts[0].astype(BF), parts[1], parts[2]
    query = head_norm(qk[:, :HD], gains[0:1, :])
    key = head_norm(qk[:, HD:], gains[1:2, :])
    value = vm[:, :HD].astype(BF)
    joined[:, HD:2 * HD] = gelu(vm[:, HD:]).astype(BF)
    joined[:, 2 * HD:] = gelu(mm).astype(BF)
    for dc in range(2):
        for dy in range(4):
            for x in range(2):
                at = (dc * 4 + dy) * PAIR + x * PIECE
                row = x * HALF + lax.rem(y + dy, 4) * PAIR + jnp.where(core == dc, 0, PIECE)
                to = pl.multiple_of(patch + row, PIECE)
                kv[0, pl.ds(to, PIECE), :] = key[at:at + PIECE, :]
                kv[1, pl.ds(to, PIECE), :] = value[at:at + PIECE, :]
    writes = []
    if last:
        writes = [pltpu.make_async_copy(kv.at[i], new_cache.at[i], sems.at[i]) for i in range(2)]
    for w in writes:
        w.start()
    queries[...] = query[:HALF, :]
    joined[HALF:, 0:HD] = attend(query[HALF:, :], kv, scores)
    for r in reads:
        r.wait()
    theirs = joined[HALF:, :]
    for j in range(D // 256):
        partial[:, j * 256:(j + 1) * 256] = jnp.dot(
            theirs, w2[:, j * 256:(j + 1) * 256], preferred_element_type=F32
        ).astype(BF)
    for w in writes:
        w.wait()


def own_body(queries, kv, joined, w2, partial, scores):
    mixed = attend(queries[...], kv, scores)
    mine = jnp.concatenate([mixed, joined[:HALF, HD:]], axis=1)
    for j in range(D // 256):
        partial[:, j * 256:(j + 1) * 256] = jnp.dot(
            mine, w2[:, j * 256:(j + 1) * 256], preferred_element_type=F32
        )


def pair_body(mine, came, *outs):
    o0, o1, o2, o3 = outs[-4:]
    o0[...] = mine[0:PAIR, :] + came[0:PAIR, :].astype(F32)
    for i, o in ((1, o1), (2, o2), (3, o3)):
        a, b = i * PAIR, (i + 1) * PAIR
        o[...] = (mine[a:b, :] + came[a:b, :].astype(F32)).astype(BF)


def column_body(mine, r1, r3, r2, factors, out):
    total = mine[...] + r1[...].astype(F32) + (r2[...].astype(F32) + r3[...].astype(F32))
    out[...] = (factors[2:3, :] * total).astype(BF)


def last_column_body(mine, r1, r3, r2, factors, here, there):
    xh, _, _ = spot()
    gate = factors[2:3, :]
    for out, at in ((here, xh), (there, 1 - xh)):
        rows = pl.ds(pl.multiple_of(at * PIECE, PIECE), PIECE)
        total = mine[rows, :] + r1[rows, :].astype(F32)
        total = total + (r2[rows, :].astype(F32) + r3[rows, :].astype(F32))
        out[...] = (gate * total).astype(BF)


def next_body(kept, p0, p1, factors, normed, own):
    xh, _, _ = spot()
    new = (kept[...].astype(F32) + (p0[...].astype(F32) + p1[...].astype(F32))).astype(BF)
    wide = new.astype(F32)
    normed[...] = layer_norm(wide, factors[...])
    own[...] = jnp.where(xh == 0, new[:PIECE, :], new[PIECE:, :])


def final_body(kept, p0, p1, out):
    out[...] = (kept[...].astype(F32) + (p0[...].astype(F32) + p1[...].astype(F32))).astype(BF)


def block(last, normed, passing, patches, w1, gains, kv, weights):
    core_parts = [send_core(normed)]
    n2 = send_y(normed, 2)
    n3 = send_y(normed, 1)
    n1 = send_y(normed, 3)
    core_parts += [send_core(p) for p in (n2, n1, n3)]
    (first,) = local_call(
        project_body,
        [("vmem", (HALF, 6 * HD), F32)],
        [("vmem", p) for p in (normed, n2, n1, n3)] + [("vmem", w1)],
        scratch=[pltpu.VMEM((HALF, D), BF)],
        flops=3_000_000_000,
        moved=5_500_000,
        name="project_own",
    )
    cache_shape = (2, TOKENS, HD)
    outs = [
        ("vmem", cache_shape, BF),
        ("vmem", (ROWS, 4 * HD), BF),
        ("vmem", (HALF, HD), BF),
        ("vmem", (HALF, D), BF),
    ]
    outs.append(("any", cache_shape, BF) if last else ("vmem", (4 * HD, D), BF))
    kind = "vmem" if last else "hbm"
    kv, joined, queries, partial, fifth = local_call(
        functools.partial(block_body, last),
        outs,
        [("smem", patches)] + [("vmem", p) for p in [first] + core_parts]
        + [("vmem", w1), ("vmem", gains), ("vmem", kv)] + [(kind, a) for a in weights],
        scratch=[
            pltpu.VMEM((HALF, D), BF),
            pltpu.VMEM((HALF, TOKENS), F32),
            pltpu.SemaphoreType.DMA((2,)),
        ],
        limit=24,
        flops=30_000_000_000,
        moved=12_000_000,
        name="block",
        aliases={8: 0},
    )
    w2 = weights[0] if last else fifth
    came = send_core(partial)
    (mine,) = local_call(
        own_body,
        [("vmem", (HALF, D), F32)],
        [("vmem", queries), ("vmem", kv), ("vmem", joined), ("vmem", w2)],
        scratch=[pltpu.VMEM((HALF, TOKENS), F32)],
        flops=12_000_000_000,
        moved=4_700_000,
        name="own_half",
    )
    o0, o1, o2, o3 = local_call(
        pair_body,
        [("vmem", (PAIR, D), F32)] + [("vmem", (PAIR, D), BF)] * 3,
        [("vmem", mine), ("vmem", came)] + [("any", p) for p in passing],
        flops=400_000,
        moved=3_000_000,
        name="pair_sum",
    )
    r2 = send_y(o2, 2)
    r1 = send_y(o1, 1)
    r3 = send_y(o3, 3)
    return (o0, r1, r3, r2), kv, fifth


def shards(
    slots,
    patch_of_slot,
    step_of_slot,
    modulation,
    w_qkv,
    qk_scale,
    w_mlp_in,
    w_attn_out,
    w_mlp_out,
    kv_cache,
):
    own = slots[0]
    other = send_x(own)
    gains = qk_scale[0]
    w1, first, second, kv = local_call(
        fetch_body,
        [
            ("vmem", (D, 6 * HD), BF),
            ("vmem", (3, D), F32),
            ("vmem", (3, D), F32),
            ("vmem", (2, TOKENS, HD), BF),
        ],
        [
            ("smem", step_of_slot),
            ("hbm", jnp.transpose(modulation[0], (1, 0, 2))),
            ("hbm", jnp.transpose(w_qkv[0], (1, 0, 2))),
            ("hbm", w_mlp_in[0]),
            ("hbm", kv_cache[0]),
        ],
        scratch=[pltpu.VMEM((3, modulation.shape[1], D), BF), pltpu.SemaphoreType.DMA((7,))],
        flops=0,
        moved=7_000_000,
        name="fetch",
    )
    factors = (first, second)

    normed, kept = local_call(
        start_body,
        [("vmem", (PAIR, D), BF)] * 2,
        [("vmem", own), ("vmem", other), ("vmem", factors[0])],
        flops=1_000_000,
        moved=400_000,
        name="norm_first",
    )
    kept = send_on(kept, 0)
    sums, kv, w2 = block(
        False, normed, (), patch_of_slot, w1, gains, kv, (w_attn_out[0], w_mlp_out[0])
    )
    (out,) = local_call(
        column_body,
        [("vmem", (PAIR, D), BF)],
        [("vmem", a) for a in sums] + [("vmem", factors[0])],
        flops=400_000,
        moved=1_200_000,
        name="column_sum",
    )
    p0, p1 = send_on(out, 0), send_on(out, 8)
    normed, kept = local_call(
        next_body,
        [("vmem", (PAIR, D), BF), ("vmem", (PIECE, D), BF)],
        [("vmem", a) for a in (kept, p0, p1, factors[1])],
        flops=1_000_000,
        moved=800_000,
        name="norm_next",
    )
    kept = send_on(kept, 0)
    sums, _, cache = block(True, normed, (kept,), patch_of_slot, w1, gains, kv, (w2,))
    here, there = local_call(
        last_column_body,
        [("vmem", (PIECE, D), BF)] * 2,
        [("vmem", a) for a in sums] + [("vmem", factors[1])],
        flops=400_000,
        moved=1_200_000,
        name="column_last",
    )
    p0, p1 = send_on(here, 0), send_on(there, 8)
    (out,) = local_call(
        final_body,
        [("hbm", (PIECE, D), BF)],
        [("vmem", a) for a in (kept, p0, p1)],
        flops=400_000,
        moved=400_000,
        name="residual_last",
    )
    return out[None], cache[None]


def solution(mesh):
    return jax.shard_map(
        shards,
        mesh=mesh,
        in_specs=(
            P("section", "sp", None),
            P(),
            P(),
            P("section", None, None, None),
            P("section", None, None, "sp"),
            P("section", None, None),
            P("section", None, "sp"),
            P("section", "sp", None),
            P("section", "sp", None),
            P("section", None, None, "sp"),
        ),
        out_specs=(P("section", "sp", None), P("section", None, None, "sp")),
        check_vma=False,
    )
```
